32 devices in a mesh: dp: 16 (over z, y, x), tensor: 2 (over core).
Axes of the slice: x: 2, y: 2, z: 4, core: 2. Of those that a mesh axis runs over, the one named last changes fastest.
Arguments:
- embeds: bfloat16 [256, 4608], P('dp'), may hold values from -6 to 6
- owner: int32 [32, 8], P('dp'), may hold values from 0 to 7, each once within a row
- pairs: int32 [32, 56, 2], P('dp'), may hold values from 0 to 7, as said below
- pref_weight: bfloat16 [2, 4608, 4608], P(None, 'dp', 'tensor'), may hold values from -0.0625 to 0.0625
- pref_bias: float32 [4608], P('tensor'), may hold values from -3 to 3
- pref_out: float32 [4608], P('tensor'), may hold values from -0.375 to 0.375
- logratio: float32 [256], P('dp'), may hold values from -3 to 3
- attn_out: bfloat16 [16384, 4096], P('dp', 'tensor'), may hold values from -6 to 6
- grad_out: bfloat16 [16384, 4608], P('dp', 'tensor'), may hold values from -6 to 6
- w_out: bfloat16 [4608, 4096], P('dp', 'tensor'), may hold values from -0.09375 to 0.09375
Outputs:
- d_attn: bfloat16 [16384, 4096], P('dp', 'tensor')
- o_grad: float32 [4608, 4096], P('dp', 'tensor')
The draws below stay inside these ranges and needn't reach their ends.
Inputs may be any that keep to these rules, and one draw needn't show every extreme that they name: `pairs`: the two numbers of a pair differ. Each row of owner names every number once.
All inputs are finite; a program needn't handle non-finite values.
Results may differ from the reference program's by a relative error of at most 0.0049.
Values may be sent and summed in bfloat16 or wider, within the bound.
A program may use at most 128 MiB of HBM per device.

```python
import jax
import jax.numpy as jnp

D = 4608
HID = 4096
PH = 4608
K = 8
NPAIR = 56
L = 64
PROMPTS = 32
RESP = 256
TOKENS = 16384


def draw_pairs(key, part):
    first_key = jax.random.fold_in(key, 11)
    step_key = jax.random.fold_in(key, 12)
    first = jax.random.randint(first_key, (PROMPTS, NPAIR), 0, K)
    step = jax.random.randint(step_key, (PROMPTS, NPAIR), 1, K)
    second = (first + step) % K
    return jnp.stack([first, second], axis=-1).astype(jnp.int32)


def block_levels(stream_key, extent, pieces, low, largest):
    factor_of, own = 1.0, jax.random.fold_in(stream_key, 6)
    for position, blocks in pieces:
        steps = jnp.exp(jax.random.uniform(jax.random.fold_in(own, position), (blocks,), jnp.float32, low / len(pieces), largest / len(pieces)))
        factor_of = factor_of * jnp.repeat(steps, extent[position] // blocks).reshape([-1 if axis == position else 1 for axis in range(len(extent))])
    return factor_of


def bell_draw(key, dims, width, limit, cuts=(), held_as=jnp.bfloat16):
    drawn = width * jax.random.normal(key, dims, jnp.float32)
    if cuts:
        drawn = drawn * block_levels(key, dims, cuts, -0.22, 0.18)
    return jnp.clip(drawn, -limit, limit).astype(held_as)


def setup_inputs(seed: int = 0) -> dict:
    key_of = jax.random.split(jax.random.key(seed), 11)
    return {
        "embeds": bell_draw(key_of[0], (RESP, D), 1.0, 6.0, ((0, 16),)),
        "owner": jax.vmap(lambda own: jax.random.permutation(own, K))(jax.random.split(key_of[1], PROMPTS)).reshape((PROMPTS, K)).astype(jnp.int32),
        "pairs": draw_pairs(jax.random.fold_in(key_of[10], 71), 0),
        "pref_weight": bell_draw(key_of[3], (2, D, PH), (2 * D) ** -0.5, 0.0625, ((1, 16), (2, 2))),
        "pref_bias": bell_draw(key_of[4], (PH,), 0.5, 3.0, ((0, 2),), jnp.float32),
        "pref_out": bell_draw(key_of[5], (PH,), (PH // 16) ** -0.5, 0.375, ((0, 2),), jnp.float32),
        "logratio": bell_draw(key_of[6], (RESP,), 0.5, 3.0, ((0, 16),), jnp.float32),
        "attn_out": bell_draw(key_of[7], (TOKENS, HID), 1.0, 6.0, ((0, 16), (1, 2))),
        "grad_out": bell_draw(key_of[8], (TOKENS, D), 1.0, 6.0, ((0, 16), (1, 2))),
        "w_out": bell_draw(key_of[9], (D, HID), HID ** -0.5, 0.09375, ((0, 16), (1, 2))),
    }


eta_scale = 2.0


def reference(embeds, owner, pairs, pref_weight, pref_bias, pref_out, logratio, attn_out, grad_out, w_out):
    upper = jnp.dot(embeds, pref_weight[0], preferred_element_type=jnp.float32)
    lower = jnp.dot(embeds, pref_weight[1], preferred_element_type=jnp.float32)
    prompts = owner.shape[0]
    base = (jnp.arange(prompts, dtype=jnp.int32) * K)[:, None]
    row_a = base + jnp.take_along_axis(owner, pairs[:, :, 0], axis=1)
    row_b = base + jnp.take_along_axis(owner, pairs[:, :, 1], axis=1)
    pre = upper[row_a] + lower[row_b] + pref_bias
    hidden = jax.nn.gelu(pre)
    logit = jnp.sum(hidden * pref_out, axis=-1)
    prob = jax.nn.sigmoid(logit)
    numbers = jnp.arange(K, dtype=jnp.int32)
    first = (pairs[:, :, 0][:, :, None] == numbers).astype(jnp.float32)
    second = (pairs[:, :, 1][:, :, None] == numbers).astype(jnp.float32)
    wins = jnp.sum(prob[:, :, None] * first + (1.0 - prob)[:, :, None] * second, axis=1)
    count = jnp.sum(first + second, axis=1)
    winrate = (wins + 1.0) / (count + 2.0)
    placed = (owner[:, :, None] == numbers).astype(jnp.float32)
    rowrate = jnp.sum(winrate[:, :, None] * placed, axis=1).reshape(-1)
    coef = 2.0 * (logratio - eta_scale * (rowrate - 0.5))
    resp = coef.shape[0]
    weighted = (grad_out.astype(jnp.float32).reshape(resp, L, -1) * coef[:, None, None]).reshape(grad_out.shape).astype(jnp.bfloat16)
    d_attn = jnp.dot(weighted, w_out, preferred_element_type=jnp.float32).astype(jnp.bfloat16)
    o_grad = jnp.dot(weighted.T, attn_out, preferred_element_type=jnp.float32) / resp
    return d_attn, o_grad
```

```python
import jax
import jax.numpy as jnp
from jax import lax
from jax.sharding import PartitionSpec as P

eta_scale = 2.0
NX = 2
NY = 2
CHUNKS = 4


def x_pairs(n):
    return [(i, i ^ 1) for i in range(n)]


def y_pairs(n):
    return [(i, i ^ NX) for i in range(n)]


def z_pairs(n, step, sign, outward):
    plane = NX * NY
    nz = n // plane
    pairs = []
    for i in range(n):
        k = i // plane
        far = k if sign > 0 else nz - 1 - k
        if far == nz - 1:
            continue
        if (far >= step - 1) if outward else (far <= step - 1):
            pairs.append((i, i + sign * plane))
    return pairs


def at(array, index):
    return lax.dynamic_index_in_dim(array, index, 0, keepdims=False)


def line_reduce(own, z, n, dtype):
    nz = own.shape[0]
    right = left = None
    for step in range(1, nz):
        give_r = at(own, jnp.clip(nz - step + z, 0, nz - 1))
        give_l = at(own, jnp.clip(z - nz + step, 0, nz - 1))
        if right is not None:
            give_r = give_r + right.astype(jnp.float32)
            give_l = give_l + left.astype(jnp.float32)
        right = lax.ppermute(give_r.astype(dtype), "dp", z_pairs(n, step, 1, False))
        left = lax.ppermute(give_l.astype(dtype), "dp", z_pairs(n, step, -1, False))
    return at(own, z) + right.astype(jnp.float32) + left.astype(jnp.float32)


def line_gather(own, z, n):
    nz = n // (NX * NY)
    rights, lefts = [], []
    right = left = own
    for step in range(1, nz):
        right = lax.ppermute(right, "dp", z_pairs(n, step, 1, True))
        left = lax.ppermute(left, "dp", z_pairs(n, step, -1, True))
        rights.append(right)
        lefts.append(left)
    line = jnp.stack(rights[::-1] + [own] + lefts)
    return lax.dynamic_slice_in_dim(line, nz - 1 - z, nz, 0)


def in_order(first, own, other, axis):
    return jnp.where(
        first,
        jnp.concatenate([own, other], axis=axis),
        jnp.concatenate([other, own], axis=axis),
    )


def shards(
    embeds, owner, pairs, pref_weight, pref_bias, pref_out, logratio, attn_out, grad_out, w_out
):
    n = lax.axis_size("dp")
    nz = n // (NX * NY)
    me = lax.axis_index("dp")
    x, y, z = me % NX, (me // NX) % NY, me // (NX * NY)
    resp_dev, width = embeds.shape
    prompts_dev, groups = owner.shape
    npairs = pairs.shape[1]
    part, hidden_local = pref_weight.shape[1:]
    tokens = grad_out.shape[0]
    half = attn_out.shape[1] // NX
    rows_out = w_out.shape[0]

    grad_other = lax.ppermute(grad_out, "dp", x_pairs(n))
    features = lax.all_gather(grad_out, "tensor", axis=1, tiled=True)
    features_other = lax.all_gather(grad_other, "tensor", axis=1, tiled=True)
    attn_mine = lax.dynamic_slice_in_dim(attn_out, x * half, half, 1)
    attn_send = lax.dynamic_slice_in_dim(attn_out, (1 - x) * half, half, 1)
    attn_other = lax.ppermute(attn_send, "dp", x_pairs(n))
    attn_both = jnp.concatenate([attn_mine, attn_other], axis=0)

    cut = embeds.reshape(resp_dev, n, part).transpose(1, 0, 2)
    cut = lax.all_to_all(cut, "dp", 0, 0, tiled=True).reshape(n * resp_dev, part)
    partial = jnp.stack(
        [
            jnp.dot(cut, pref_weight[s], preferred_element_type=jnp.float32)
            for s in range(2)
        ],
        axis=1,
    ).reshape(nz, NY, NX, resp_dev, 2, hidden_local)
    keep = lax.dynamic_index_in_dim(partial, y, 1, keepdims=False)
    send = lax.dynamic_index_in_dim(partial, 1 - y, 1, keepdims=False)
    keep = keep + lax.ppermute(send, "dp", y_pairs(n))
    keep = line_reduce(keep, z, n, jnp.float32)
    both = at(keep, x) + lax.ppermute(at(keep, 1 - x), "dp", x_pairs(n))
    upper, lower = both[:, 0], both[:, 1]

    base = (jnp.arange(prompts_dev, dtype=jnp.int32) * groups)[:, None]
    row_a = base + jnp.take_along_axis(owner, pairs[:, :, 0], axis=1)
    row_b = base + jnp.take_along_axis(owner, pairs[:, :, 1], axis=1)
    pre = upper[row_a.reshape(-1)] + lower[row_b.reshape(-1)]
    pre = pre.reshape(prompts_dev, npairs, hidden_local)
    hidden = jax.nn.gelu(pre + pref_bias)
    logit = lax.psum(jnp.sum(hidden * pref_out, axis=-1), "tensor")
    prob = jax.nn.sigmoid(logit)
    numbers = jnp.arange(groups, dtype=jnp.int32)
    first = (pairs[:, :, 0][:, :, None] == numbers).astype(jnp.float32)
    second = (pairs[:, :, 1][:, :, None] == numbers).astype(jnp.float32)
    wins = jnp.sum(prob[:, :, None] * first + (1.0 - prob)[:, :, None] * second, axis=1)
    count = jnp.sum(first + second, axis=1)
    winrate = (wins + 1.0) / (count + 2.0)
    placed = (owner[:, :, None] == numbers).astype(jnp.float32)
    rowrate = jnp.sum(winrate[:, :, None] * placed, axis=1).reshape(-1)
    coef = 2.0 * (logratio - eta_scale * (rowrate - 0.5))
    coef_other = lax.ppermute(coef, "dp", x_pairs(n))

    def scale(block, by):
        shaped = block.astype(jnp.float32).reshape(resp_dev, -1, width)
        return (shaped * by[:, None, None]).reshape(block.shape).astype(jnp.bfloat16)

    weighted = jnp.concatenate([scale(features, coef), scale(features_other, coef_other)], axis=0)

    w_other = lax.ppermute(
        lax.dynamic_slice_in_dim(w_out, (1 - x) * half, half, 1), "dp", x_pairs(n)
    )
    w_mine = lax.dynamic_slice_in_dim(w_out, x * half, half, 1)
    w_pair = in_order(x == 0, w_mine, w_other, 0)
    w_line = line_gather(w_pair, z, n)
    w_line_other = lax.ppermute(w_line, "dp", y_pairs(n))
    w_all = in_order(y == 0, w_line[:, None], w_line_other[:, None], 1).reshape(-1, half)

    step = half // CHUNKS
    pieces = []
    for c in range(CHUNKS):
        block = lax.dot_general(
            weighted,
            attn_both[:, c * step : (c + 1) * step],
            (((0,), (0,)), ((), ())),
            preferred_element_type=jnp.float32,
        ).reshape(nz, NY, NX * rows_out, step)
        mine = lax.dynamic_index_in_dim(block, y, 1, keepdims=False)
        away = lax.dynamic_index_in_dim(block, 1 - y, 1, keepdims=False).astype(jnp.bfloat16)
        mine = mine + lax.ppermute(away, "dp", y_pairs(n)).astype(jnp.float32)
        pieces.append(line_reduce(mine, z, n, jnp.bfloat16))

    d_send = jnp.dot(weighted[tokens:], w_all, preferred_element_type=jnp.float32).astype(
        jnp.bfloat16
    )
    d_other = lax.ppermute(d_send, "dp", x_pairs(n))
    d_mine = jnp.dot(weighted[:tokens], w_all, preferred_element_type=jnp.float32).astype(
        jnp.bfloat16
    )
    d_attn = in_order(x == 0, d_mine, d_other, 1)

    total_resp = resp_dev * n
    summed = jnp.concatenate(pieces, axis=1).reshape(NX, rows_out, half)
    o_other = lax.ppermute(at(summed, 1 - x).astype(jnp.bfloat16), "dp", x_pairs(n))
    o_grad = in_order(x == 0, at(summed, x), o_other.astype(jnp.float32), 1) / total_resp
    return (d_attn, o_grad)


def solution(mesh):
    return jax.shard_map(
        shards,
        mesh=mesh,
        in_specs=(
            P("dp", None),
            P("dp", None),
            P("dp", None, None),
            P(None, "dp", "tensor"),
            P("tensor"),
            P("tensor"),
            P("dp"),
            P("dp", "tensor"),
            P("dp", "tensor"),
            P("dp", "tensor"),
        ),
        out_specs=(P("dp", "tensor"), P("dp", "tensor")),
        check_vma=False,
    )
```

```python
import jax
import jax.numpy as jnp
from jax import lax
from jax.sharding import PartitionSpec as P

eta_scale = 2.0
NX = 2
NY = 2
CHUNKS = 4


def x_pairs(n):
    return [(i, i ^ 1) for i in range(n)]


def y_pairs(n):
    return [(i, i ^ NX) for i in range(n)]


def z_pairs(n, step, sign, outward):
    plane = NX * NY
    nz = n // plane
    pairs = []
    for i in range(n):
        k = i // plane
        far = k if sign > 0 else nz - 1 - k
        if far == nz - 1:
            continue
        if (far >= step - 1) if outward else (far <= step - 1):
            pairs.append((i, i + sign * plane))
    return pairs


def at(array, index):
    return lax.dynamic_index_in_dim(array, index, 0, keepdims=False)


def line_reduce(own, z, n, dtype):
    nz = own.shape[0]
    right = left = None
    for step in range(1, nz):
        give_r = at(own, jnp.clip(nz - step + z, 0, nz - 1))
        give_l = at(own, jnp.clip(z - nz + step, 0, nz - 1))
        if right is not None:
            give_r = give_r + right.astype(jnp.float32)
            give_l = give_l + left.astype(jnp.float32)
        right = lax.ppermute(give_r.astype(dtype), "dp", z_pairs(n, step, 1, False))
        left = lax.ppermute(give_l.astype(dtype), "dp", z_pairs(n, step, -1, False))
    return at(own, z) + right.astype(jnp.float32) + left.astype(jnp.float32)


def line_gather(own, z, n):
    nz = n // (NX * NY)
    rights, lefts = [], []
    right = left = own
    for step in range(1, nz):
        right = lax.ppermute(right, "dp", z_pairs(n, step, 1, True))
        left = lax.ppermute(left, "dp", z_pairs(n, step, -1, True))
        rights.append(right)
        lefts.append(left)
    line = jnp.stack(rights[::-1] + [own] + lefts)
    return lax.dynamic_slice_in_dim(line, nz - 1 - z, nz, 0)


def after(value, *others):
    return lax.optimization_barrier((value,) + others)[0]


def in_order(first, own, other, axis):
    return jnp.where(
        first,
        jnp.concatenate([own, other], axis=axis),
        jnp.concatenate([other, own], axis=axis),
    )


def project(block, *parts):
    return jnp.concatenate(
        [
            jnp.dot(block, part, preferred_element_type=jnp.float32).astype(jnp.bfloat16)
            for part in parts
        ],
        axis=1,
    )


def shards(
    embeds, owner, pairs, pref_weight, pref_bias, pref_out, logratio, attn_out, grad_out, w_out
):
    n = lax.axis_size("dp")
    nz = n // (NX * NY)
    me = lax.axis_index("dp")
    x, y, z = me % NX, (me // NX) % NY, me // (NX * NY)
    resp_dev, width = embeds.shape
    prompts_dev, groups = owner.shape
    npairs = pairs.shape[1]
    part, hidden_local = pref_weight.shape[1:]
    tokens = grad_out.shape[0]
    half = attn_out.shape[1] // NX
    rows_out = w_out.shape[0]

    grad_other = lax.ppermute(grad_out, "dp", x_pairs(n))
    features = lax.all_gather(grad_out, "tensor", axis=1, tiled=True)
    features_other = lax.all_gather(grad_other, "tensor", axis=1, tiled=True)
    attn_mine = lax.dynamic_slice_in_dim(attn_out, x * half, half, 1)
    attn_send = lax.dynamic_slice_in_dim(attn_out, (1 - x) * half, half, 1)
    attn_other = lax.ppermute(after(attn_send, grad_other), "dp", x_pairs(n))
    attn_both = jnp.concatenate([attn_mine, attn_other], axis=0)

    cut = embeds.reshape(resp_dev, n, part).transpose(1, 0, 2)
    cut = lax.all_to_all(cut, "dp", 0, 0, tiled=True).reshape(n * resp_dev, part)
    partial = jnp.stack(
        [
            jnp.dot(cut, pref_weight[s], preferred_element_type=jnp.float32)
            for s in range(2)
        ],
        axis=1,
    ).reshape(nz, NY, NX, resp_dev, 2, hidden_local)
    keep = lax.dynamic_index_in_dim(partial, y, 1, keepdims=False)
    send = lax.dynamic_index_in_dim(partial, 1 - y, 1, keepdims=False)
    got = lax.ppermute(send, "dp", y_pairs(n))
    keep = line_reduce(keep + got, z, n, jnp.float32)
    both = at(keep, x) + lax.ppermute(at(keep, 1 - x), "dp", x_pairs(n))
    upper, lower = both[:, 0], both[:, 1]

    base = (jnp.arange(prompts_dev, dtype=jnp.int32) * groups)[:, None]
    row_a = base + jnp.take_along_axis(owner, pairs[:, :, 0], axis=1)
    row_b = base + jnp.take_along_axis(owner, pairs[:, :, 1], axis=1)
    pre = upper[row_a.reshape(-1)] + lower[row_b.reshape(-1)]
    pre = pre.reshape(prompts_dev, npairs, hidden_local)
    hidden = jax.nn.gelu(pre + pref_bias)
    logit = lax.psum(jnp.sum(hidden * pref_out, axis=-1), "tensor")
    prob = jax.nn.sigmoid(logit)
    numbers = jnp.arange(groups, dtype=jnp.int32)
    first = (pairs[:, :, 0][:, :, None] == numbers).astype(jnp.float32)
    second = (pairs[:, :, 1][:, :, None] == numbers).astype(jnp.float32)
    wins = jnp.sum(prob[:, :, None] * first + (1.0 - prob)[:, :, None] * second, axis=1)
    count = jnp.sum(first + second, axis=1)
    winrate = (wins + 1.0) / (count + 2.0)
    placed = (owner[:, :, None] == numbers).astype(jnp.float32)
    rowrate = jnp.sum(winrate[:, :, None] * placed, axis=1).reshape(-1)
    coef = 2.0 * (logratio - eta_scale * (rowrate - 0.5))
    coef_other = lax.ppermute(coef, "dp", x_pairs(n))

    def scale(block, by):
        shaped = block.astype(jnp.float32).reshape(resp_dev, -1, width)
        return (shaped * by[:, None, None]).reshape(block.shape).astype(jnp.bfloat16)

    weighted = jnp.concatenate([scale(features, coef), scale(features_other, coef_other)], axis=0)

    w_send = lax.dynamic_slice_in_dim(w_out, (1 - x) * half, half, 1)
    w_other = lax.ppermute(after(w_send, send), "dp", x_pairs(n))
    w_mine = lax.dynamic_slice_in_dim(w_out, x * half, half, 1)
    w_pair = in_order(x == 0, w_mine, w_other, 0)
    w_a, w_b = w_pair[:, : half // 2], w_pair[:, half // 2 :]
    w_a = line_gather(w_a, z, n)
    w_a_other = lax.ppermute(after(w_a, got), "dp", y_pairs(n))
    w_a = in_order(y == 0, w_a[:, None], w_a_other[:, None], 1).reshape(-1, half // 2)
    w_b_other = lax.ppermute(after(w_b, got), "dp", y_pairs(n))
    w_b = in_order(y == 0, w_b[None], w_b_other[None], 0)
    w_b = line_gather(after(w_b, keep), z, n).reshape(-1, half // 2)

    step = half // CHUNKS
    pieces = []
    came = None
    d_attn = None
    for c in range(CHUNKS):
        block = lax.dot_general(
            weighted,
            attn_both[:, c * step : (c + 1) * step],
            (((0,), (0,)), ((), ())),
            preferred_element_type=jnp.float32,
        ).reshape(nz, NY, NX * rows_out, step)
        mine = lax.dynamic_index_in_dim(block, y, 1, keepdims=False)
        away = lax.dynamic_index_in_dim(block, 1 - y, 1, keepdims=False).astype(jnp.bfloat16)
        if came is not None:
            away = after(away, came)
        came = lax.ppermute(away, "dp", y_pairs(n))
        if c == 0:
            w_a, w_b, _ = lax.optimization_barrier((w_a, w_b, came))
            d_other = lax.ppermute(project(weighted[tokens:], w_a, w_b), "dp", x_pairs(n))
            d_mine = project(weighted[:tokens], w_a, w_b)
            d_attn = in_order(x == 0, d_mine, d_other, 1)
        if c == CHUNKS - 1:
            came, d_attn = lax.optimization_barrier((came, d_attn))
        pieces.append(line_reduce(mine + came.astype(jnp.float32), z, n, jnp.bfloat16))

    total_resp = resp_dev * n
    summed = jnp.concatenate(pieces, axis=1).reshape(NX, rows_out, half)
    o_other = lax.ppermute(at(summed, 1 - x).astype(jnp.bfloat16), "dp", x_pairs(n))
    o_grad = in_order(x == 0, at(summed, x), o_other.astype(jnp.float32), 1) / total_resp
    return (d_attn, o_grad)


def solution(mesh):
    return jax.shard_map(
        shards,
        mesh=mesh,
        in_specs=(
            P("dp", None),
            P("dp", None),
            P("dp", None, None),
            P(None, "dp", "tensor"),
            P("tensor"),
            P("tensor"),
            P("dp"),
            P("dp", "tensor"),
            P("dp", "tensor"),
            P("dp", "tensor"),
        ),
        out_specs=(P("dp", "tensor"), P("dp", "tensor")),
        check_vma=False,
    )
```

```python
import jax
import jax.numpy as jnp
from jax import lax
from jax.sharding import PartitionSpec as P

eta_scale = 2.0
NX = 2
NY = 2
CHUNKS = (3, 2, 2, 1)


def x_pairs(n):
    return [(i, i ^ 1) for i in range(n)]


def y_pairs(n):
    return [(i, i ^ NX) for i in range(n)]


def z_pairs(n, step, sign, outward):
    plane = NX * NY
    nz = n // plane
    pairs = []
    for i in range(n):
        k = i // plane
        far = k if sign > 0 else nz - 1 - k
        if far == nz - 1:
            continue
        if (far >= step - 1) if outward else (far <= step - 1):
            pairs.append((i, i + sign * plane))
    return pairs


def at(array, index):
    return lax.dynamic_index_in_dim(array, index, 0, keepdims=False)


def after(value, *others):
    marks = tuple(other[(slice(0, 1),) * other.ndim] for other in others)
    return lax.optimization_barrier((value,) + marks)[0]


def line_reduce(own, z, n, dtype):
    nz = own.shape[0]
    right = left = None
    for step in range(1, nz):
        give_r = at(own, jnp.clip(nz - step + z, 0, nz - 1))
        give_l = at(own, jnp.clip(z - nz + step, 0, nz - 1))
        if right is not None:
            give_r = give_r + right.astype(jnp.float32)
            give_l = give_l + left.astype(jnp.float32)
        right = lax.ppermute(give_r.astype(dtype), "dp", z_pairs(n, step, 1, False))
        left = lax.ppermute(give_l.astype(dtype), "dp", z_pairs(n, step, -1, False))
    return at(own, z) + right.astype(jnp.float32) + left.astype(jnp.float32)


def line_gather(own, z, n, gates=None):
    nz = n // (NX * NY)
    rights, lefts = [], []
    right = left = own
    for step in range(1, nz):
        right = lax.ppermute(right, "dp", z_pairs(n, step, 1, True))
        left = lax.ppermute(left, "dp", z_pairs(n, step, -1, True))
        if gates and step in gates:
            right, left = after(right, gates[step]), after(left, gates[step])
        rights.append(right)
        lefts.append(left)
    line = jnp.stack(rights[::-1] + [own] + lefts)
    return lax.dynamic_slice_in_dim(line, nz - 1 - z, nz, 0)


def in_order(first, own, other, axis):
    return jnp.where(
        first,
        jnp.concatenate([own, other], axis=axis),
        jnp.concatenate([other, own], axis=axis),
    )


def project(block, *parts):
    return jnp.concatenate(
        [
            jnp.dot(block, part, preferred_element_type=jnp.float32).astype(jnp.bfloat16)
            for part in parts
        ],
        axis=1,
    )


def shards(
    embeds, owner, pairs, pref_weight, pref_bias, pref_out, logratio, attn_out, grad_out, w_out
):
    n = lax.axis_size("dp")
    nz = n // (NX * NY)
    me = lax.axis_index("dp")
    x, y, z = me % NX, (me // NX) % NY, me // (NX * NY)
    resp_dev, width = embeds.shape
    prompts_dev, groups = owner.shape
    npairs = pairs.shape[1]
    part, hidden_local = pref_weight.shape[1:]
    tokens = grad_out.shape[0]
    half = attn_out.shape[1] // NX
    rows_out = w_out.shape[0]

    grad_other = lax.ppermute(grad_out, "dp", x_pairs(n))
    features = lax.all_gather(grad_out, "tensor", axis=1, tiled=True)
    attn_mine = lax.dynamic_slice_in_dim(attn_out, x * half, half, 1)
    attn_send = lax.dynamic_slice_in_dim(attn_out, (1 - x) * half, half, 1)

    cut = embeds.reshape(resp_dev, n, part).transpose(1, 0, 2)
    cut = lax.all_to_all(cut, "dp", 0, 0, tiled=True).reshape(n * resp_dev, part)
    partial = jnp.stack(
        [
            jnp.dot(cut, pref_weight[s], preferred_element_type=jnp.float32)
            for s in range(2)
        ],
        axis=1,
    ).reshape(nz, NY, NX, resp_dev, 2, hidden_local)
    keep = lax.dynamic_index_in_dim(partial, y, 1, keepdims=False)
    send = lax.dynamic_index_in_dim(partial, 1 - y, 1, keepdims=False)
    got = lax.ppermute(send, "dp", y_pairs(n))
    keep = line_reduce(keep + got, z, n, jnp.float32)
    last = lax.ppermute(at(keep, 1 - x), "dp", x_pairs(n))
    both = at(keep, x) + last
    features_other = lax.all_gather(after(grad_other, last), "tensor", axis=1, tiled=True)
    attn_other = lax.ppermute(after(attn_send, last), "dp", x_pairs(n))
    attn_both = jnp.concatenate([attn_mine, attn_other], axis=0)
    upper, lower = both[:, 0], both[:, 1]

    base = (jnp.arange(prompts_dev, dtype=jnp.int32) * groups)[:, None]
    row_a = base + jnp.take_along_axis(owner, pairs[:, :, 0], axis=1)
    row_b = base + jnp.take_along_axis(owner, pairs[:, :, 1], axis=1)
    pre = upper[row_a.reshape(-1)] + lower[row_b.reshape(-1)]
    pre = pre.reshape(prompts_dev, npairs, hidden_local)
    hidden = jax.nn.gelu(pre + pref_bias)
    logit = lax.psum(jnp.sum(hidden * pref_out, axis=-1), "tensor")
    prob = jax.nn.sigmoid(logit)
    numbers = jnp.arange(groups, dtype=jnp.int32)
    first = (pairs[:, :, 0][:, :, None] == numbers).astype(jnp.float32)
    second = (pairs[:, :, 1][:, :, None] == numbers).astype(jnp.float32)
    wins = jnp.sum(prob[:, :, None] * first + (1.0 - prob)[:, :, None] * second, axis=1)
    count = jnp.sum(first + second, axis=1)
    winrate = (wins + 1.0) / (count + 2.0)
    placed = (owner[:, :, None] == numbers).astype(jnp.float32)
    rowrate = jnp.sum(winrate[:, :, None] * placed, axis=1).reshape(-1)
    coef = 2.0 * (logratio - eta_scale * (rowrate - 0.5))
    coef_other = lax.ppermute(coef, "dp", x_pairs(n))

    def scale(block, by):
        shaped = block.astype(jnp.float32).reshape(resp_dev, -1, width)
        return (shaped * by[:, None, None]).reshape(block.shape).astype(jnp.bfloat16)

    weighted = jnp.concatenate([scale(features, coef), scale(features_other, coef_other)], axis=0)

    w_send = lax.dynamic_slice_in_dim(w_out, (1 - x) * half, half, 1)
    w_other = lax.ppermute(after(w_send, send), "dp", x_pairs(n))
    w_mine = lax.dynamic_slice_in_dim(w_out, x * half, half, 1)
    w_pair = in_order(x == 0, w_mine, w_other, 0)
    w_a, w_b = w_pair[:, : half // 2], w_pair[:, half // 2 :]
    w_a = line_gather(w_a, z, n)
    w_a_other = lax.ppermute(after(w_a, got), "dp", y_pairs(n))
    w_a = in_order(y == 0, w_a[:, None], w_a_other[:, None], 1).reshape(-1, half // 2)
    w_b_other = lax.ppermute(after(w_b, got), "dp", y_pairs(n))
    w_b = in_order(y == 0, w_b[None], w_b_other[None], 0)

    unit = half // sum(CHUNKS)
    pieces = []
    arrivals = []
    begin = 0
    d_attn = None
    for c, units in enumerate(CHUNKS):
        step = units * unit
        block = lax.dot_general(
            weighted,
            attn_both[:, begin : begin + step],
            (((0,), (0,)), ((), ())),
            preferred_element_type=jnp.float32,
        ).reshape(nz, NY, NX * rows_out, step)
        mine = lax.dynamic_index_in_dim(block, y, 1, keepdims=False)
        away = lax.dynamic_index_in_dim(block, 1 - y, 1, keepdims=False).astype(jnp.bfloat16)
        begin += step
        if c >= 2:
            away = after(away, arrivals[c - 2])
        came = lax.ppermute(away, "dp", y_pairs(n))
        arrivals.append(came)
        if c == 0:
            gates = {1: last, nz - 2: weighted, nz - 1: came}
            w_a = after(w_a, came)
            w_b = line_gather(after(w_b, keep), z, n, gates).reshape(-1, half // 2)
            d_other = lax.ppermute(project(weighted[tokens:], w_a, w_b), "dp", x_pairs(n))
            d_mine = project(weighted[:tokens], w_a, w_b)
            d_attn = in_order(x == 0, d_mine, d_other, 1)
        if c == len(CHUNKS) - 1:
            came, d_attn = lax.optimization_barrier((came, d_attn))
        pieces.append(line_reduce(mine + came.astype(jnp.float32), z, n, jnp.bfloat16))

    total_resp = resp_dev * n
    summed = jnp.concatenate(pieces, axis=1).reshape(NX, rows_out, half)
    o_other = lax.ppermute(at(summed, 1 - x).astype(jnp.bfloat16), "dp", x_pairs(n))
    o_grad = in_order(x == 0, at(summed, x), o_other.astype(jnp.float32), 1) / total_resp
    return (d_attn, o_grad)


def solution(mesh):
    return jax.shard_map(
        shards,
        mesh=mesh,
        in_specs=(
            P("dp", None),
            P("dp", None),
            P("dp", None, None),
            P(None, "dp", "tensor"),
            P("tensor"),
            P("tensor"),
            P("dp"),
            P("dp", "tensor"),
            P("dp", "tensor"),
            P("dp", "tensor"),
        ),
        out_specs=(P("dp", "tensor"), P("dp", "tensor")),
        check_vma=False,
    )
```

```python
import jax
import jax.numpy as jnp
from jax import lax
from jax.sharding import PartitionSpec as P

eta_scale = 2.0
NX = 2
NY = 2
CHUNKS = (1, 1, 1, 1)


def x_pairs(n):
    return [(i, i ^ 1) for i in range(n)]


def y_pairs(n):
    return [(i, i ^ NX) for i in range(n)]


def z_pairs(n, step, sign, outward):
    plane = NX * NY
    nz = n // plane
    pairs = []
    for i in range(n):
        k = i // plane
        far = k if sign > 0 else nz - 1 - k
        if far == nz - 1:
            continue
        if (far >= step - 1) if outward else (far <= step - 1):
            pairs.append((i, i + sign * plane))
    return pairs


def at(array, index):
    return lax.dynamic_index_in_dim(array, index, 0, keepdims=False)


def after(value, *others):
    marks = tuple(other[(slice(0, 1),) * other.ndim] for other in others)
    return lax.optimization_barrier((value,) + marks)[0]


def line_reduce(own, z, n, dtype):
    nz = own.shape[0]
    right = left = None
    for step in range(1, nz):
        give_r = at(own, jnp.clip(nz - step + z, 0, nz - 1))
        give_l = at(own, jnp.clip(z - nz + step, 0, nz - 1))
        if right is not None:
            give_r = give_r + right.astype(jnp.float32)
            give_l = give_l + left.astype(jnp.float32)
        right = lax.ppermute(give_r.astype(dtype), "dp", z_pairs(n, step, 1, False))
        left = lax.ppermute(give_l.astype(dtype), "dp", z_pairs(n, step, -1, False))
    return at(own, z) + right.astype(jnp.float32) + left.astype(jnp.float32)


def line_gather(own, z, n, gates=None):
    nz = n // (NX * NY)
    rights, lefts = [], []
    right = left = own
    for step in range(1, nz):
        right = lax.ppermute(right, "dp", z_pairs(n, step, 1, True))
        left = lax.ppermute(left, "dp", z_pairs(n, step, -1, True))
        if gates and step in gates:
            right, left = after(right, gates[step]), after(left, gates[step])
        rights.append(right)
        lefts.append(left)
    line = jnp.stack(rights[::-1] + [own] + lefts)
    return lax.dynamic_slice_in_dim(line, nz - 1 - z, nz, 0)


def in_order(first, own, other, axis):
    return jnp.where(
        first,
        jnp.concatenate([own, other], axis=axis),
        jnp.concatenate([other, own], axis=axis),
    )


def project(block, *parts):
    return jnp.concatenate(
        [
            jnp.dot(block, part, preferred_element_type=jnp.float32).astype(jnp.bfloat16)
            for part in parts
        ],
        axis=1,
    )


def shards(
    embeds, owner, pairs, pref_weight, pref_bias, pref_out, logratio, attn_out, grad_out, w_out
):
    n = lax.axis_size("dp")
    nz = n // (NX * NY)
    me = lax.axis_index("dp")
    x, y, z = me % NX, (me // NX) % NY, me // (NX * NY)
    resp_dev, width = embeds.shape
    prompts_dev, groups = owner.shape
    npairs = pairs.shape[1]
    part, hidden_local = pref_weight.shape[1:]
    tokens = grad_out.shape[0]
    half = attn_out.shape[1] // NX
    rows_out = w_out.shape[0]

    features = lax.all_gather(grad_out, "tensor", axis=1, tiled=True)
    attn_mine = lax.dynamic_slice_in_dim(attn_out, x * half, half, 1)
    attn_send = lax.dynamic_slice_in_dim(attn_out, (1 - x) * half, half, 1)

    cut = embeds.reshape(resp_dev, n, part).transpose(1, 0, 2)
    cut = lax.all_to_all(cut, "dp", 0, 0, tiled=True).reshape(n * resp_dev, part)
    partial = jnp.stack(
        [
            jnp.dot(cut, pref_weight[s], preferred_element_type=jnp.float32)
            for s in range(2)
        ],
        axis=1,
    ).reshape(nz, NY, NX, resp_dev, 2, hidden_local)
    keep = lax.dynamic_index_in_dim(partial, y, 1, keepdims=False)
    send = lax.dynamic_index_in_dim(partial, 1 - y, 1, keepdims=False)
    got = lax.ppermute(send, "dp", y_pairs(n))
    keep = line_reduce(keep + got, z, n, jnp.float32)
    last = lax.ppermute(at(keep, 1 - x), "dp", x_pairs(n))
    both = at(keep, x) + last
    upper, lower = both[:, 0], both[:, 1]

    base = (jnp.arange(prompts_dev, dtype=jnp.int32) * groups)[:, None]
    row_a = base + jnp.take_along_axis(owner, pairs[:, :, 0], axis=1)
    row_b = base + jnp.take_along_axis(owner, pairs[:, :, 1], axis=1)
    pre = upper[row_a.reshape(-1)] + lower[row_b.reshape(-1)]
    pre = pre.reshape(prompts_dev, npairs, hidden_local)
    hidden = jax.nn.gelu(pre + pref_bias)
    logit = lax.psum(jnp.sum(hidden * pref_out, axis=-1), "tensor")
    prob = jax.nn.sigmoid(logit)
    numbers = jnp.arange(groups, dtype=jnp.int32)
    first = (pairs[:, :, 0][:, :, None] == numbers).astype(jnp.float32)
    second = (pairs[:, :, 1][:, :, None] == numbers).astype(jnp.float32)
    wins = jnp.sum(prob[:, :, None] * first + (1.0 - prob)[:, :, None] * second, axis=1)
    count = jnp.sum(first + second, axis=1)
    winrate = (wins + 1.0) / (count + 2.0)
    placed = (owner[:, :, None] == numbers).astype(jnp.float32)
    rowrate = jnp.sum(winrate[:, :, None] * placed, axis=1).reshape(-1)
    coef = 2.0 * (logratio - eta_scale * (rowrate - 0.5))
    coef_other = lax.ppermute(coef, "dp", x_pairs(n))

    def scale(block, by):
        shaped = block.astype(jnp.float32).reshape(resp_dev, -1, width)
        return (shaped * by[:, None, None]).reshape(block.shape).astype(jnp.bfloat16)

    w_send = lax.dynamic_slice_in_dim(w_out, (1 - x) * half, half, 1)
    w_other = lax.ppermute(after(w_send, send), "dp", x_pairs(n))
    grad_other = lax.ppermute(after(grad_out, w_other), "dp", x_pairs(n))
    w_mine = lax.dynamic_slice_in_dim(w_out, x * half, half, 1)
    w_pair = in_order(x == 0, w_mine, w_other, 0)
    w_a, w_b = w_pair[:, : half // 2], w_pair[:, half // 2 :]
    w_a = line_gather(w_a, z, n)
    w_b_other = lax.ppermute(after(w_b, got), "dp", y_pairs(n))
    w_a_other = lax.ppermute(after(w_a, w_b_other), "dp", y_pairs(n))
    w_a = in_order(y == 0, w_a[:, None], w_a_other[:, None], 1).reshape(-1, half // 2)
    w_b = in_order(y == 0, w_b[None], w_b_other[None], 0)

    features_other = lax.all_gather(after(grad_other, last), "tensor", axis=1, tiled=True)
    attn_other = lax.ppermute(after(attn_send, last), "dp", x_pairs(n))
    attn_both = jnp.concatenate([attn_mine, attn_other], axis=0)
    weighted = jnp.concatenate([scale(features, coef), scale(features_other, coef_other)], axis=0)

    unit = half // sum(CHUNKS)
    pieces = []
    arrivals = []
    begin = 0
    d_attn = None
    for c, units in enumerate(CHUNKS):
        step = units * unit
        block = lax.dot_general(
            weighted,
            attn_both[:, begin : begin + step],
            (((0,), (0,)), ((), ())),
            preferred_element_type=jnp.float32,
        ).reshape(nz, NY, NX * rows_out, step)
        mine = lax.dynamic_index_in_dim(block, y, 1, keepdims=False)
        away = lax.dynamic_index_in_dim(block, 1 - y, 1, keepdims=False).astype(jnp.bfloat16)
        begin += step
        if c >= 1:
            away = after(away, arrivals[c - 1])
        came = lax.ppermute(away, "dp", y_pairs(n))
        arrivals.append(came)
        if c == 0:
            gates = {1: last, nz - 2: weighted, nz - 1: came}
            w_a = after(w_a, came)
            w_b = line_gather(after(w_b, keep), z, n, gates).reshape(-1, half // 2)
            d_other = lax.ppermute(project(weighted[tokens:], w_a, w_b), "dp", x_pairs(n))
            d_mine = project(weighted[:tokens], w_a, w_b)
            d_attn = in_order(x == 0, d_mine, d_other, 1)
        if c == len(CHUNKS) - 1:
            came, d_attn = lax.optimization_barrier((came, d_attn))
        pieces.append(line_reduce(mine + came.astype(jnp.float32), z, n, jnp.bfloat16))

    total_resp = resp_dev * n
    summed = jnp.concatenate(pieces, axis=1).reshape(NX, rows_out, half)
    o_other = lax.ppermute(at(summed, 1 - x).astype(jnp.bfloat16), "dp", x_pairs(n))
    o_grad = in_order(x == 0, at(summed, x), o_other.astype(jnp.float32), 1) / total_resp
    return (d_attn, o_grad)


def solution(mesh):
    return jax.shard_map(
        shards,
        mesh=mesh,
        in_specs=(
            P("dp", None),
            P("dp", None),
            P("dp", None, None),
            P(None, "dp", "tensor"),
            P("tensor"),
            P("tensor"),
            P("dp"),
            P("dp", "tensor"),
            P("dp", "tensor"),
            P("dp", "tensor"),
        ),
        out_specs=(P("dp", "tensor"), P("dp", "tensor")),
        check_vma=False,
    )
```
